128 devices in a mesh: tm: 8 (over y, core), tile: 16 (over z, x).
Axes of the slice: x: 4, y: 4, z: 4, core: 2. Of those that a mesh axis runs over, the one named last changes fastest.
Arguments:
- latents: bfloat16 [48, 16, 64, 128], P('tm', 'tile'), may hold values from -6 to 6
- group_frames: int32 [8], P('tm'), may hold values from 4 to 6, as said below
- conv_in_weight: bfloat16 [3, 3, 3, 16, 512], replicated, may hold values from -0.3125 to 0.3125
- conv_weight: bfloat16 [3, 3, 3, 512, 256], replicated, may hold values from -0.0546875 to 0.0546875
- shortcut_weight: bfloat16 [512, 256], replicated, may hold values from -0.25 to 0.25
- bias_out: float32 [256], replicated, may hold values from -3 to 3
Outputs:
- decoded: bfloat16 [48, 64, 128, 256], P('tm', 'tile')
The draws below stay inside these ranges and needn't reach their ends.
Inputs may be any that keep to these rules, and one draw needn't show every extreme that they name: `group_frames`: live frames of each group, which form the clip in group order; some group holds 6 and some holds 4 in every draw.
All inputs are finite; a program needn't handle non-finite values.
Results may differ from the reference program's by a relative error of at most 0.0051.
Values may be sent and summed in bfloat16 or wider, within the bound.
A program may use at most 64 MiB of HBM per device.

```python
import jax
import jax.numpy as jnp
from jax import lax

LC = 16
HID = 512
OUT = 256
W = 128
FMAX = 6
H = 64
SLOTS = 48
N_TM = 8


def draw_group_frames(key, part):
    key = jax.random.fold_in(key, 11)
    first_key, second_key = jax.random.split(key)
    counts = jax.random.randint(first_key, (N_TM,), 4, FMAX + 1)
    order = jax.random.permutation(second_key, N_TM)
    counts = counts.at[order[0]].set(FMAX)
    counts = counts.at[order[1]].set(4)
    return counts.astype(jnp.int32)


def level_of(key, shape, pieces, least, high):
    def one(axis_at, shards_of):
        draws = jax.random.uniform(jax.random.fold_in(jax.random.fold_in(key, 6), axis_at), (shards_of,), jnp.float32, least / len(pieces), high / len(pieces))
        return jnp.repeat(jnp.exp(draws), shape[axis_at] // shards_of).reshape((-1,) + (1,) * (len(shape) - axis_at - 1))

    level = one(*pieces[0])
    for cut in pieces[1:]:
        level = level * one(*cut)
    return level


def noise(stream_key, extent, spread, most, cuts=(), held_as=jnp.bfloat16):
    result = spread * jax.random.normal(stream_key, extent, jnp.float32)
    if cuts:
        result = result * level_of(stream_key, extent, cuts, -0.22, 0.18)
    return jnp.clip(result, -most, most).astype(held_as)


def setup_inputs(seed: int = 0) -> dict:
    arg_keys = jax.random.split(jax.random.key(seed), 7)
    latents = noise(arg_keys[0], (SLOTS, LC, H, W), 1.0, 6.0, ((0, 8), (1, 16)))
    group_frames = draw_group_frames(jax.random.fold_in(arg_keys[6], 71), 0)
    conv_in_weight = noise(arg_keys[2], (3, 3, 3, LC, HID), (27 * LC) ** -0.5, 0.3125)
    conv_weight = noise(arg_keys[3], (3, 3, 3, HID, OUT), (27 * HID) ** -0.5, 0.0546875)
    shortcut_weight = noise(arg_keys[4], (HID, OUT), HID ** -0.5, 0.25)
    bias_out = noise(arg_keys[5], (OUT,), 0.5, 3.0, (), jnp.float32)
    return {"latents": latents, "group_frames": group_frames, "conv_in_weight": conv_in_weight, "conv_weight": conv_weight, "shortcut_weight": shortcut_weight, "bias_out": bias_out}


def reference(latents, group_frames, conv_in_weight, conv_weight, shortcut_weight, bias_out):
    groups = latents.reshape(N_TM, FMAX, LC, H, W)
    in_matrix = conv_in_weight.astype(jnp.float32).reshape(27 * LC, HID)
    block_weight = conv_weight.astype(jnp.float32)
    short_matrix = shortcut_weight.astype(jnp.float32)

    def one_group(group_id):
        current = lax.dynamic_index_in_dim(groups, group_id, 0, keepdims=False)
        earlier_id = jnp.maximum(group_id - 1, 0).astype(jnp.int32)
        previous = lax.dynamic_index_in_dim(groups, earlier_id, 0, keepdims=False)
        prev_len = group_frames[earlier_id]
        context = lax.dynamic_slice_in_dim(previous, (prev_len - 4).astype(jnp.int32), 4, 0)
        context = jnp.where(group_id == 0, jnp.broadcast_to(current[:1], context.shape), context)
        window = jnp.concatenate([context, current], 0)
        window = jnp.pad(window, ((0, 0), (0, 0), (1, 1), (1, 1)), mode="edge").astype(jnp.float32)
        tap_list = [window[step_t:step_t + FMAX + 2, :, step_r:step_r + H, step_c:step_c + W]
                    for step_t in range(3) for step_r in range(3) for step_c in range(3)]
        stacked = jnp.stack(tap_list, 1).reshape(FMAX + 2, 27 * LC, H, W)
        hidden = jnp.einsum("fkrw,kd->frwd", stacked, in_matrix).astype(jnp.bfloat16)
        activated = jax.nn.silu(hidden.astype(jnp.float32)).astype(jnp.bfloat16)
        padded = jnp.pad(activated, ((0, 0), (1, 1), (1, 1), (0, 0)), mode="edge").astype(jnp.float32)
        total_sum = jnp.zeros((FMAX, H, W, OUT), jnp.float32)
        for step_t in range(3):
            for step_r in range(3):
                for step_c in range(3):
                    piece = padded[step_t:step_t + FMAX, step_r:step_r + H, step_c:step_c + W]
                    total_sum = total_sum + jnp.einsum("frwc,cd->frwd", piece, block_weight[step_t, step_r, step_c])
        total_sum = total_sum + jnp.einsum("frwc,cd->frwd", hidden[2:].astype(jnp.float32), short_matrix)
        total_sum = total_sum + bias_out.astype(jnp.float32)
        live_mask = jnp.arange(FMAX) < group_frames[group_id]
        return jnp.where(live_mask[:, None, None, None], total_sum, 0.0).astype(jnp.bfloat16)

    decoded = lax.map(one_group, jnp.arange(N_TM).astype(jnp.int32))
    return decoded.reshape(N_TM * FMAX, H, W, OUT)
```

```python
import functools

import jax
import jax.numpy as jnp
import numpy as np
from jax import lax
from jax.experimental import pallas as pl
from jax.experimental.pallas import tpu as pltpu
from jax.sharding import PartitionSpec as P

MESH = pl.DeviceIdType.MESH
F32, BF16 = jnp.float32, jnp.bfloat16

FRAMES = 6
BACK = 4
LC, HID, OUT = 16, 512, 256
H, W = 64, 128
BAND = 4
WIN = BAND + 4


def in_weight_order():
    order = np.zeros((512, 27 * LC), np.float32)
    for a in range(3):
        for q in range(LC):
            for s in range(8):
                e, b = divmod(s, 3)
                order[a * 128 + q * 8 + s, ((a * 3 + b) * 3 + e) * LC + q] = 1
            order[384 + q * 8 + 7 - a, ((a * 3 + 2) * 3 + 2) * LC + q] = 1
    return order


def exchange_kernel(n_tm, n_tile, gf_ref, lat_ref, win_ref, order_ref, cw_ref,
                    own_ref, prev_ref, u_ref, wp_ref,
                    pad, s_own, s_next, r_own, r_prev, wbuf, ubuf,
                    send_sem, recv_sem, w_sem, u_sem):
    k, j = lax.axis_index("tm"), lax.axis_index("tile")
    last = n_tm - 1
    barrier = pltpu.get_barrier_semaphore()

    def greet(s, _):
        pl.semaphore_signal(barrier, inc=1, device_id={"tile": lax.rem(j + s, n_tile)}, device_id_type=MESH)
        return 0

    lax.fori_loop(1, n_tile, greet, 0)

    @pl.when(k > 0)
    def _():
        def greet_before(s, _):
            pl.semaphore_signal(
                barrier, inc=1, device_id={"tm": k - 1, "tile": lax.rem(j + s, n_tile)}, device_id_type=MESH
            )
            return 0

        lax.fori_loop(0, n_tile, greet_before, 0)

    def w_copy(c):
        return pltpu.make_async_copy(cw_ref.at[:, c], wbuf.at[c], w_sem.at[c])

    for c in range(9):
        w_copy(c).start()

    lat = lat_ref[...].astype(F32)
    pad[BACK:, 2:H + 2] = lat
    for row in (0, 1):
        pad[BACK:, row:row + 1] = lat[:, :1]
        pad[BACK:, H + 2 + row:H + 3 + row] = lat[:, H - 1:]
    start = jnp.clip(gf_ref[0] - BACK, 0, FRAMES - BACK) + BACK
    for f in range(BACK):
        pad[f] = pad[start + f]
    for i in range(n_tile):
        rows = pad[:, BAND * i:BAND * i + WIN]
        s_next[i] = rows[:BACK].reshape(BACK * WIN, W).astype(BF16)
        s_own[i] = rows[BACK:].reshape(FRAMES * WIN, W).astype(BF16)

    pl.semaphore_wait(barrier, n_tile - 1 + jnp.where(k < last, n_tile, 0))

    def own_copy(s):
        to = lax.rem(j + s, n_tile)
        return pltpu.make_async_remote_copy(
            src_ref=s_own.at[to], dst_ref=r_own.at[j], send_sem=send_sem.at[s], recv_sem=recv_sem.at[s],
            device_id={"tile": to}, device_id_type=MESH)

    def next_copy(s):
        to = lax.rem(j + s, n_tile)
        return pltpu.make_async_remote_copy(
            src_ref=s_next.at[to], dst_ref=r_prev.at[j], send_sem=send_sem.at[n_tile + s],
            recv_sem=recv_sem.at[n_tile + s], device_id={"tm": k + 1, "tile": to}, device_id_type=MESH)

    def run(first, fn):
        def body(s, _):
            fn(s)
            return 0

        lax.fori_loop(first, n_tile, body, 0)

    run(1, lambda s: own_copy(s).start())

    @pl.when(k < last)
    def _():
        run(0, lambda s: next_copy(s).start())

    r_own[j] = s_own[j]

    def u_copy(c):
        return pltpu.make_async_copy(ubuf.at[c], u_ref.at[:, c], u_sem.at[c])

    def prepare(c, _):
        w_copy(c).wait()
        for part in range(4):
            rows = pl.ds(part * 128, 128)
            g0, g1, g2 = (wbuf[c, a, rows].astype(F32) for a in range(3))
            even, odd = 0.5 * (g0 + g2), 0.5 * g1
            ubuf[c, 0, rows] = (even + odd).astype(BF16)
            ubuf[c, 1, rows] = (even - odd).astype(BF16)
        u_copy(c).start()
        return 0

    lax.fori_loop(0, 9, prepare, 0)
    wp_ref[...] = jnp.dot(order_ref[...], win_ref[...], preferred_element_type=F32).astype(BF16)

    run(1, lambda s: own_copy(s).wait_recv())
    own_ref[...] = r_own[...]

    @pl.when(k > 0)
    def _():
        run(0, lambda s: next_copy(s).wait_recv())
        prev_ref[...] = r_prev[...]

    @pl.when(k == 0)
    def _():
        prev_ref[...] = jnp.zeros_like(prev_ref)

    run(1, lambda s: own_copy(s).wait_send())

    @pl.when(k < last)
    def _():
        run(0, lambda s: next_copy(s).wait_send())

    def drain(c, _):
        u_copy(c).wait()
        return 0

    lax.fori_loop(0, 9, drain, 0)


def exchange(n_tm, n_tile, group_frames, latents, win, order, cw):
    vmem = pl.BlockSpec(memory_space=pltpu.VMEM)
    hbm = pl.BlockSpec(memory_space=pltpu.HBM)
    return pl.pallas_call(
        functools.partial(exchange_kernel, n_tm, n_tile),
        out_shape=(
            jax.ShapeDtypeStruct((LC, FRAMES * WIN, W), BF16),
            jax.ShapeDtypeStruct((LC, BACK * WIN, W), BF16),
            jax.ShapeDtypeStruct((2, 9, HID, OUT), BF16),
            jax.ShapeDtypeStruct((512, HID), BF16),
        ),
        in_specs=[pl.BlockSpec(memory_space=pltpu.SMEM), vmem, vmem, vmem, hbm],
        out_specs=(vmem, vmem, hbm, vmem),
        scratch_shapes=[
            pltpu.VMEM((BACK + FRAMES, H + 8, W), F32),
            pltpu.VMEM((n_tile, FRAMES * WIN, W), BF16),
            pltpu.VMEM((n_tile, BACK * WIN, W), BF16),
            pltpu.VMEM((LC, FRAMES * WIN, W), BF16),
            pltpu.VMEM((LC, BACK * WIN, W), BF16),
            pltpu.VMEM((9, 3, HID, OUT), BF16),
            pltpu.VMEM((9, 2, HID, OUT), BF16),
            pltpu.SemaphoreType.DMA((2 * n_tile,)),
            pltpu.SemaphoreType.DMA((2 * n_tile,)),
            pltpu.SemaphoreType.DMA((9,)),
            pltpu.SemaphoreType.DMA((9,)),
        ],
        compiler_params=pltpu.CompilerParams(
            collective_id=0, has_side_effects=True, vmem_limit_bytes=40 << 20
        ),
        name="exchange",
    )(group_frames, latents, win, order, cw)


def block_kernel(n_tile, gf_ref, own_ref, prev_ref, wp_ref, cw_ref, u_ref, short_ref, bias_ref, out_ref,
                 main, turned, hid, v, wts, y, staged, w_sem, o_sem):
    k, j = lax.axis_index("tm"), lax.axis_index("tile")
    own_len = gf_ref[0]

    def w_copy(i, e):
        src = (cw_ref.at[0], u_ref.at[0], u_ref.at[1], cw_ref.at[2])[i]
        return pltpu.make_async_copy(src.at[:, e], wts.at[e, i], w_sem.at[e, i])

    for e in range(3):
        for i in range(4):
            w_copy(i, e).start()

    slot = lax.broadcasted_iota(jnp.int32, (128, 128), 1) % 8

    def lanes(x, shift):
        shift = shift % 128
        return pltpu.roll(x, shift, 1) if shift else x

    def spread(f, planes):
        mid = planes.reshape(LC * WIN, W).T
        left = jnp.concatenate([mid[:1], mid[:-1]], 0)
        right = jnp.concatenate([mid[1:], mid[-1:]], 0)
        for r in range(9):
            t2 = lanes(right, 6 - r)
            turned[f, r] = t2.astype(BF16)
            if r < 6:
                taps = jnp.where(slot < 3, lanes(left, -r), jnp.where(slot < 6, lanes(mid, 3 - r), t2))
                main[f, r] = taps.astype(BF16)

    first = own_ref[:, 0:16].astype(F32)[:, :WIN]
    for g in range(2):
        pair = prev_ref[:, 16 * g:16 * g + 16].astype(F32)
        for h in range(2):
            spread(2 * g + h, jnp.where(k == 0, first, pair[:, h * WIN:(h + 1) * WIN]))
    for g in range(3):
        pair = own_ref[:, 16 * g:16 * g + 16].astype(F32)
        for h in range(2):
            spread(BACK + 2 * g + h, pair[:, h * WIN:(h + 1) * WIN])

    low, high = jnp.where(j == 0, 1, 0), jnp.where(j == n_tile - 1, BAND, BAND + 1)
    slot16 = slot.astype(F32).astype(BF16)

    def row_step(r, _):
        src = jnp.clip(r, low, high)
        acts = []
        for t in range(8):
            rest = jnp.where(slot == 7, turned[t, src + 1].astype(F32),
                             jnp.where(slot == 6, turned[t + 1, src + 2].astype(F32),
                                       turned[t + 2, src + 3].astype(F32))).astype(BF16)
            taps = jnp.concatenate([main[t, src], main[t + 1, src], main[t + 2, src], rest], 1)
            hidden = jnp.dot(taps, wp_ref[...], preferred_element_type=F32).astype(BF16)
            if t >= 2:
                hid[t - 2, r] = hidden
            half = hidden.astype(F32) * 0.5
            acts.append((half + half * jnp.tanh(half)).astype(BF16))
        for tau in range(3):
            d0, d1, d2, d3 = acts[2 * tau:2 * tau + 4]
            v[tau, 0, r] = d0 - d2
            v[tau, 1, r] = d1 + d2
            v[tau, 2, r] = d2 - d1
            v[tau, 3, r] = d1 - d3
        return 0

    lax.fori_loop(0, 6, row_step, 0)

    for e in range(3):
        for i in range(4):
            w_copy(i, e).wait()

    def o_copy(tau):
        frames = pl.ds(2 * tau, 2)
        return pltpu.make_async_copy(staged.at[frames], out_ref.at[frames], o_sem.at[tau])

    def pair_step(tau, _):
        def tap_step(e, _):
            m = []
            for i in range(4):
                total = None
                for b in range(3):
                    lhs = v[tau, i, b:b + BAND].reshape(BAND * W, HID)
                    part = jnp.dot(lhs, wts[e, i, b], preferred_element_type=F32)
                    total = part if total is None else total + part
                m.append(total)
            y[e, 0] = m[0] + m[1] + m[2]
            y[e, 1] = m[1] - m[2] - m[3]
            return 0

        lax.fori_loop(0, 3, tap_step, 0)
        for p in range(2):
            t = 2 * tau + p
            live = t < own_len
            for r in range(BAND):
                rows = pl.ds(r * W, W)
                y0, y2 = y[0, p, rows], y[2, p, rows]
                total = jnp.dot(hid[t, 1 + r], short_ref[...], preferred_element_type=F32) + bias_ref[...]
                total += y[1, p, rows]
                total += jnp.concatenate([y0[:1], y0[:-1]], 0)
                total += jnp.concatenate([y2[1:], y2[-1:]], 0)
                staged[t, r] = jnp.where(live, total, 0.0).astype(BF16)
        o_copy(tau).start()
        return 0

    lax.fori_loop(0, 3, pair_step, 0)
    for tau in range(3):
        o_copy(tau).wait()


def block(n_tile, group_frames, own, prev, wp, cw, u, short, bias):
    vmem = pl.BlockSpec(memory_space=pltpu.VMEM)
    hbm = pl.BlockSpec(memory_space=pltpu.HBM)
    return pl.pallas_call(
        functools.partial(block_kernel, n_tile),
        out_shape=jax.ShapeDtypeStruct((FRAMES, BAND, W, OUT), BF16),
        in_specs=[pl.BlockSpec(memory_space=pltpu.SMEM), vmem, vmem, vmem, hbm, hbm, vmem, vmem],
        out_specs=hbm,
        scratch_shapes=[
            pltpu.VMEM((BACK + FRAMES, 6, 128, 128), BF16),
            pltpu.VMEM((BACK + FRAMES, 9, 128, 128), BF16),
            pltpu.VMEM((FRAMES, 6, W, HID), BF16),
            pltpu.VMEM((3, 4, 6, W, HID), BF16),
            pltpu.VMEM((3, 4, 3, HID, OUT), BF16),
            pltpu.VMEM((3, 2, BAND * W, OUT), F32),
            pltpu.VMEM((FRAMES, BAND, W, OUT), BF16),
            pltpu.SemaphoreType.DMA((3, 4)),
            pltpu.SemaphoreType.DMA((3,)),
        ],
        compiler_params=pltpu.CompilerParams(vmem_limit_bytes=52 << 20),
        name="block",
    )(group_frames, own, prev, wp, cw, u, short, bias)


def per_device(n_tm, n_tile, latents, group_frames, conv_in_weight, conv_weight, shortcut_weight, bias_out):
    order = jnp.asarray(in_weight_order(), BF16)
    own, prev, u, wp = exchange(
        n_tm, n_tile, group_frames, latents.reshape(FRAMES, H, W), conv_in_weight.reshape(27 * LC, HID),
        order, conv_weight.reshape(3, 9, HID, OUT))
    return block(
        n_tile, group_frames, own, prev, wp, conv_weight.reshape(3, 3, 3, HID, OUT),
        u.reshape(2, 3, 3, HID, OUT), shortcut_weight, bias_out.reshape(1, OUT))


def solution(mesh):
    in_specs = (P("tm", "tile", None, None), P("tm"), P(), P(), P(), P())
    out_specs = P("tm", "tile", None, None)
    return jax.shard_map(
        functools.partial(per_device, mesh.shape["tm"], mesh.shape["tile"]),
        mesh=mesh, in_specs=in_specs, out_specs=out_specs, check_vma=False,
    )
```

```python
import functools

import jax
import jax.numpy as jnp
import numpy as np
from jax import lax
from jax.experimental import pallas as pl
from jax.experimental.pallas import tpu as pltpu
from jax.sharding import PartitionSpec as P

MESH = pl.DeviceIdType.MESH
F32, BF16 = jnp.float32, jnp.bfloat16

FRAMES = 6
BACK = 4
LC, HID, OUT = 16, 512, 256
H, W = 64, 128
BAND = 4
WIN = BAND + 4


def in_weight_order():
    order = np.zeros((512, 27 * LC), np.float32)
    for a in range(3):
        for q in range(LC):
            for s in range(8):
                e, b = divmod(s, 3)
                order[a * 128 + q * 8 + s, ((a * 3 + b) * 3 + e) * LC + q] = 1
            order[384 + q * 8 + 7 - a, ((a * 3 + 2) * 3 + 2) * LC + q] = 1
    return order


def time_row_weights(g):
    def three(x0, x1, x2):
        even, odd = 0.5 * (x0 + x2), 0.5 * x1
        return x0, even + odd, even - odd, x2

    columns = [three(g[0][b], g[1][b], g[2][b]) for b in range(3)]
    return [three(columns[0][i], columns[1][i], columns[2][i]) for i in range(4)]


def exchange_kernel(n_tm, n_tile, gf_ref, lat_ref, win_ref, order_ref, cw_ref,
                    own_ref, prev_ref, u_ref, wp_ref,
                    lat_buf, win_buf, order_buf, pad, s_own, s_next, r_own, r_prev, wbuf,
                    send_sem, recv_sem, w_sem, in_sem):
    k, j = lax.axis_index("tm"), lax.axis_index("tile")
    last = n_tm - 1
    barrier = pltpu.get_barrier_semaphore()

    lat_copy = pltpu.make_async_copy(lat_ref, lat_buf, in_sem.at[0])
    win_copy = pltpu.make_async_copy(win_ref, win_buf, in_sem.at[1])
    order_copy = pltpu.make_async_copy(order_ref, order_buf, in_sem.at[2])
    lat_copy.start()

    def greet(s, _):
        pl.semaphore_signal(barrier, inc=1, device_id={"tile": lax.rem(j + s, n_tile)}, device_id_type=MESH)
        return 0

    lax.fori_loop(1, n_tile, greet, 0)

    @pl.when(k > 0)
    def _():
        def greet_before(s, _):
            pl.semaphore_signal(
                barrier, inc=1, device_id={"tm": k - 1, "tile": lax.rem(j + s, n_tile)}, device_id_type=MESH
            )
            return 0

        lax.fori_loop(0, n_tile, greet_before, 0)

    def w_copy(e):
        return pltpu.make_async_copy(cw_ref.at[:, :, e], wbuf.at[e], w_sem.at[e])

    win_copy.start()
    order_copy.start()
    for e in range(3):
        w_copy(e).start()

    lat_copy.wait()
    lat = lat_buf[...].astype(F32)
    pad[BACK:, 2:H + 2] = lat
    for row in (0, 1):
        pad[BACK:, row:row + 1] = lat[:, :1]
        pad[BACK:, H + 2 + row:H + 3 + row] = lat[:, H - 1:]
    start = jnp.clip(gf_ref[0] - BACK, 0, FRAMES - BACK) + BACK
    for f in range(BACK):
        pad[f] = pad[start + f]
    for i in range(n_tile):
        rows = pad[:, BAND * i:BAND * i + WIN]
        s_next[i] = rows[:BACK].reshape(BACK * WIN, W).astype(BF16)
        s_own[i] = rows[BACK:].reshape(FRAMES * WIN, W).astype(BF16)

    pl.semaphore_wait(barrier, n_tile - 1 + jnp.where(k < last, n_tile, 0))

    def own_copy(s):
        to = lax.rem(j + s, n_tile)
        return pltpu.make_async_remote_copy(
            src_ref=s_own.at[to], dst_ref=r_own.at[j], send_sem=send_sem.at[s], recv_sem=recv_sem.at[s],
            device_id={"tile": to}, device_id_type=MESH)

    def next_copy(s):
        to = lax.rem(j + s, n_tile)
        return pltpu.make_async_remote_copy(
            src_ref=s_next.at[to], dst_ref=r_prev.at[j], send_sem=send_sem.at[n_tile + s],
            recv_sem=recv_sem.at[n_tile + s], device_id={"tm": k + 1, "tile": to}, device_id_type=MESH)

    def run(first, fn):
        def body(s, _):
            fn(s)
            return 0

        lax.fori_loop(first, n_tile, body, 0)

    run(1, lambda s: own_copy(s).start())

    @pl.when(k < last)
    def _():
        run(0, lambda s: next_copy(s).start())

    r_own[j] = s_own[j]

    win_copy.wait()
    order_copy.wait()
    wp_ref[...] = jnp.dot(order_buf[...], win_buf[...], preferred_element_type=F32).astype(BF16)

    def prepare(e, _):
        w_copy(e).wait()

        def part(n, _):
            rows = pl.ds(pl.multiple_of(n * 32, 32), 32)
            g = [[wbuf[e, a, b, rows].astype(F32) for b in range(3)] for a in range(3)]
            made = time_row_weights(g)
            for i in range(4):
                for jj in range(4):
                    u_ref[e, 4 * i + jj, rows] = made[i][jj].astype(BF16)
            return 0

        lax.fori_loop(0, HID // 32, part, 0)
        return 0

    lax.fori_loop(0, 3, prepare, 0)

    run(1, lambda s: own_copy(s).wait_recv())
    own_ref[...] = r_own[...]

    @pl.when(k > 0)
    def _():
        run(0, lambda s: next_copy(s).wait_recv())
        prev_ref[...] = r_prev[...]

    @pl.when(k == 0)
    def _():
        prev_ref[...] = jnp.zeros_like(prev_ref)

    run(1, lambda s: own_copy(s).wait_send())

    @pl.when(k < last)
    def _():
        run(0, lambda s: next_copy(s).wait_send())


def in_hbm(x):
    return pltpu.with_memory_space_constraint(x, pltpu.HBM)


def in_vmem(x):
    return pltpu.with_memory_space_constraint(x, pltpu.VMEM)


def exchange(n_tm, n_tile, group_frames, latents, win, order, cw):
    vmem = pl.BlockSpec(memory_space=pltpu.VMEM)
    hbm = pl.BlockSpec(memory_space=pltpu.HBM)
    return pl.pallas_call(
        functools.partial(exchange_kernel, n_tm, n_tile),
        out_shape=(
            pltpu.VMEM((LC, FRAMES * WIN, W), BF16),
            pltpu.VMEM((LC, BACK * WIN, W), BF16),
            pltpu.VMEM((3, 16, HID, OUT), BF16),
            pltpu.VMEM((512, HID), BF16),
        ),
        in_specs=[pl.BlockSpec(memory_space=pltpu.SMEM), hbm, hbm, hbm, hbm],
        out_specs=(vmem, vmem, vmem, vmem),
        scratch_shapes=[
            pltpu.VMEM((FRAMES, H, W), BF16),
            pltpu.VMEM((27 * LC, HID), BF16),
            pltpu.VMEM((512, 27 * LC), BF16),
            pltpu.VMEM((BACK + FRAMES, H + 8, W), F32),
            pltpu.VMEM((n_tile, FRAMES * WIN, W), BF16),
            pltpu.VMEM((n_tile, BACK * WIN, W), BF16),
            pltpu.VMEM((LC, FRAMES * WIN, W), BF16),
            pltpu.VMEM((LC, BACK * WIN, W), BF16),
            pltpu.VMEM((3, 3, 3, HID, OUT), BF16),
            pltpu.SemaphoreType.DMA((2 * n_tile,)),
            pltpu.SemaphoreType.DMA((2 * n_tile,)),
            pltpu.SemaphoreType.DMA((3,)),
            pltpu.SemaphoreType.DMA((3,)),
        ],
        compiler_params=pltpu.CompilerParams(
            collective_id=0, has_side_effects=True, vmem_limit_bytes=20 << 20
        ),
        name="exchange",
    )(group_frames, in_hbm(latents), in_hbm(win), in_hbm(order), in_hbm(cw))


def block_kernel(n_tile, gf_ref, own_ref, prev_ref, wp_ref, u_ref, short_hbm, bias_hbm, out_ref,
                 main, turned, hid, act, va, vb, staged, short_ref, bias_ref, in_sem, o_sem):
    k, j = lax.axis_index("tm"), lax.axis_index("tile")
    own_len = gf_ref[0]
    short_copy = pltpu.make_async_copy(short_hbm, short_ref, in_sem.at[0])
    bias_copy = pltpu.make_async_copy(bias_hbm, bias_ref, in_sem.at[1])
    short_copy.start()
    bias_copy.start()

    slot = lax.broadcasted_iota(jnp.int32, (128, 128), 1) % 8

    def lanes(x, shift):
        shift = shift % 128
        return pltpu.roll(x, shift, 1) if shift else x

    def spread(f, planes):
        mid = planes.reshape(LC * WIN, W).T
        left = jnp.concatenate([mid[:1], mid[:-1]], 0)
        right = jnp.concatenate([mid[1:], mid[-1:]], 0)
        for r in range(9):
            t2 = lanes(right, 6 - r)
            turned[f, r] = t2.astype(BF16)
            if r < 6:
                taps = jnp.where(slot < 3, lanes(left, -r), jnp.where(slot < 6, lanes(mid, 3 - r), t2))
                main[f, r] = taps.astype(BF16)

    first = own_ref[:, 0:16].astype(F32)[:, :WIN]
    for g in range(2):
        pair = prev_ref[:, 16 * g:16 * g + 16].astype(F32)
        for h in range(2):
            spread(2 * g + h, jnp.where(k == 0, first, pair[:, h * WIN:(h + 1) * WIN]))
    for g in range(3):
        pair = own_ref[:, 16 * g:16 * g + 16].astype(F32)
        for h in range(2):
            spread(BACK + 2 * g + h, pair[:, h * WIN:(h + 1) * WIN])

    low, high = jnp.where(j == 0, 1, 0), jnp.where(j == n_tile - 1, BAND, BAND + 1)

    def row_step(r, _):
        src = jnp.clip(r, low, high)
        for t in range(8):
            rest = jnp.where(slot == 7, turned[t, src + 1].astype(F32),
                             jnp.where(slot == 6, turned[t + 1, src + 2].astype(F32),
                                       turned[t + 2, src + 3].astype(F32))).astype(BF16)
            taps = jnp.concatenate([main[t, src], main[t + 1, src], main[t + 2, src], rest], 1)
            hidden = jnp.dot(taps, wp_ref[...], preferred_element_type=F32).astype(BF16)
            if t >= 2:
                hid[t - 2, r] = hidden
            half = hidden.astype(F32) * 0.5
            act[r, t] = (half + half * jnp.tanh(half)).astype(BF16)
        return 0

    lax.fori_loop(0, 6, row_step, 0)

    def turn_part(tau, rho, to, rows):
        def four(x):
            return x[0] - x[2], x[1] + x[2], x[2] - x[1], x[1] - x[3]

        planes = [[act[2 * rho + b, 2 * tau + a, rows].astype(F32) for a in range(4)] for b in range(4)]
        in_time = [four(planes[b]) for b in range(4)]
        for i in range(4):
            for jj, made in enumerate(four([in_time[b][i] for b in range(4)])):
                to[4 * i + jj, rows] = made.astype(BF16)

    PARTS = W // 16

    def part_rows(n):
        return pl.ds(n * 16, 16)

    def tile_step(tau, rho, frm, next_tau, next_rho, to):
        total = [[None, None], [None, None]]
        done = 0
        for e in range(3):
            rows_out = []
            for i in range(4):
                m = []
                for jj in range(4):
                    m.append(jnp.dot(frm[4 * i + jj], u_ref[e, 4 * i + jj], preferred_element_type=F32))
                rows_out.append(((m[1] + m[2]) + m[0], (m[1] - m[2]) - m[3]))
                step = 4 * e + i + 1
                while done * 12 < step * PARTS and done < PARTS:
                    turn_part(next_tau, next_rho, to, part_rows(done))
                    done += 1
            for q in range(2):
                s = [x[q] for x in rows_out]
                for p, y in enumerate((s[0] + s[1] + s[2], s[1] - s[2] - s[3])):
                    if e == 0:
                        y = jnp.concatenate([y[:1], y[:-1]], 0)
                    if e == 2:
                        y = jnp.concatenate([y[1:], y[-1:]], 0)
                    total[p][q] = y if e == 0 else total[p][q] + y
        for p in range(2):
            t = 2 * tau + p
            for q in range(2):
                r = 2 * rho + q
                y = total[p][q] + jnp.dot(hid[t, 1 + r], short_ref[...], preferred_element_type=F32) + bias_ref[...]
                staged[t, r] = jnp.where(t < own_len, y, 0.0).astype(BF16)

    def o_copy(tau):
        frames = pl.ds(2 * tau, 2)
        return pltpu.make_async_copy(staged.at[frames], out_ref.at[frames], o_sem.at[tau])

    for n in range(PARTS):
        turn_part(0, 0, va, part_rows(n))
    short_copy.wait()
    bias_copy.wait()

    def pair_step(tau, _):
        tile_step(tau, 0, va, tau, 1, vb)
        tile_step(tau, 1, vb, jnp.minimum(tau + 1, 2), 0, va)
        o_copy(tau).start()
        return 0

    lax.fori_loop(0, 3, pair_step, 0)
    for tau in range(3):
        o_copy(tau).wait()


def block(n_tile, group_frames, own, prev, wp, u, short, bias):
    vmem = pl.BlockSpec(memory_space=pltpu.VMEM)
    hbm = pl.BlockSpec(memory_space=pltpu.HBM)
    return pl.pallas_call(
        functools.partial(block_kernel, n_tile),
        out_shape=jax.ShapeDtypeStruct((FRAMES, BAND, W, OUT), BF16),
        in_specs=[pl.BlockSpec(memory_space=pltpu.SMEM), vmem, vmem, vmem, vmem, hbm, hbm],
        out_specs=hbm,
        scratch_shapes=[
            pltpu.VMEM((BACK + FRAMES, 6, 128, 128), BF16),
            pltpu.VMEM((BACK + FRAMES, 9, 128, 128), BF16),
            pltpu.VMEM((FRAMES, 6, W, HID), BF16),
            pltpu.VMEM((6, 8, W, HID), BF16),
            pltpu.VMEM((16, W, HID), BF16),
            pltpu.VMEM((16, W, HID), BF16),
            pltpu.VMEM((FRAMES, BAND, W, OUT), BF16),
            pltpu.VMEM((HID, OUT), BF16),
            pltpu.VMEM((1, OUT), F32),
            pltpu.SemaphoreType.DMA((2,)),
            pltpu.SemaphoreType.DMA((3,)),
        ],
        compiler_params=pltpu.CompilerParams(vmem_limit_bytes=44 << 20),
        name="block",
    )(group_frames, in_vmem(own), in_vmem(prev), in_vmem(wp), in_vmem(u), in_hbm(short), in_hbm(bias))


def per_device(n_tm, n_tile, latents, group_frames, conv_in_weight, conv_weight, shortcut_weight, bias_out):
    order = jnp.asarray(in_weight_order(), BF16)
    own, prev, u, wp = exchange(
        n_tm, n_tile, group_frames, latents.reshape(FRAMES, H, W), conv_in_weight.reshape(27 * LC, HID),
        order, conv_weight)
    return block(n_tile, group_frames, own, prev, wp, u, shortcut_weight, bias_out.reshape(1, OUT))


def solution(mesh):
    in_specs = (P("tm", "tile", None, None), P("tm"), P(), P(), P(), P())
    out_specs = P("tm", "tile", None, None)
    return jax.shard_map(
        functools.partial(per_device, mesh.shape["tm"], mesh.shape["tile"]),
        mesh=mesh, in_specs=in_specs, out_specs=out_specs, check_vma=False,
    )
```

```python
import functools

import jax
import jax.numpy as jnp
import numpy as np
from jax import lax
from jax.experimental import pallas as pl
from jax.experimental.pallas import tpu as pltpu
from jax.sharding import PartitionSpec as P

MESH = pl.DeviceIdType.MESH
F32, BF16 = jnp.float32, jnp.bfloat16

FRAMES = 6
BACK = 4
LC, HID, OUT = 16, 512, 256
H, W = 64, 128
BAND = 4
WIN = BAND + 4


def in_weight_order():
    order = np.zeros((512, 27 * LC), np.float32)
    for a in range(3):
        for q in range(LC):
            for s in range(8):
                e, b = divmod(s, 3)
                order[a * 128 + q * 8 + s, ((a * 3 + b) * 3 + e) * LC + q] = 1
            order[384 + q * 8 + 7 - a, ((a * 3 + 2) * 3 + 2) * LC + q] = 1
    return order


def time_row_weights(g):
    def three(x0, x1, x2):
        even, odd = 0.5 * (x0 + x2), 0.5 * x1
        return x0, even + odd, even - odd, x2

    columns = [three(g[0][b], g[1][b], g[2][b]) for b in range(3)]
    return [three(columns[0][i], columns[1][i], columns[2][i]) for i in range(4)]


def exchange_kernel(n_tm, n_tile, gf_ref, lat_ref, win_ref, order_ref, cw_ref,
                    own_ref, prev_ref, u_ref, wp_ref,
                    lat_buf, win_buf, order_buf, pad, s_own, s_next, r_own, r_prev, wbuf,
                    send_sem, recv_sem, w_sem, in_sem):
    k, j = lax.axis_index("tm"), lax.axis_index("tile")
    last = n_tm - 1
    barrier = pltpu.get_barrier_semaphore()

    lat_copy = pltpu.make_async_copy(lat_ref, lat_buf, in_sem.at[0])
    win_copy = pltpu.make_async_copy(win_ref, win_buf, in_sem.at[1])
    order_copy = pltpu.make_async_copy(order_ref, order_buf, in_sem.at[2])
    lat_copy.start()

    def greet(to):
        pl.semaphore_signal(barrier, inc=1, device_id=to, device_id_type=MESH)

    peers = [lax.rem(j + s, n_tile) for s in range(n_tile)]
    for to in peers[1:]:
        greet({"tile": to})

    @pl.when(k > 0)
    def _():
        for to in peers:
            greet({"tm": k - 1, "tile": to})

    def w_copy(e):
        return pltpu.make_async_copy(cw_ref.at[:, :, e], wbuf.at[e], w_sem.at[e])

    win_copy.start()
    order_copy.start()
    for e in range(3):
        w_copy(e).start()

    lat_copy.wait()
    lat = lat_buf[...].astype(F32)
    pad[BACK:, 2:H + 2] = lat
    for row in (0, 1):
        pad[BACK:, row:row + 1] = lat[:, :1]
        pad[BACK:, H + 2 + row:H + 3 + row] = lat[:, H - 1:]
    start = jnp.clip(gf_ref[0] - BACK, 0, FRAMES - BACK) + BACK
    for f in range(BACK):
        pad[f] = pad[start + f]
    for i in range(n_tile):
        rows = pad[:, BAND * i:BAND * i + WIN]
        s_next[i] = rows[:BACK].reshape(BACK * WIN, W).astype(BF16)
        s_own[i] = rows[BACK:].reshape(FRAMES * WIN, W).astype(BF16)

    pl.semaphore_wait(barrier, n_tile - 1 + jnp.where(k < last, n_tile, 0))

    def own_copy(src, dst, to):
        return pltpu.make_async_remote_copy(
            src_ref=src, dst_ref=dst, send_sem=send_sem.at[0], recv_sem=recv_sem.at[0],
            device_id={"tile": to}, device_id_type=MESH)

    def next_copy(src, dst, to):
        return pltpu.make_async_remote_copy(
            src_ref=src, dst_ref=dst, send_sem=send_sem.at[1], recv_sem=recv_sem.at[1],
            device_id={"tm": k + 1, "tile": to}, device_id_type=MESH)

    for to in peers[1:]:
        own_copy(s_own.at[to], r_own.at[j], to).start()

    @pl.when(k < last)
    def _():
        for to in peers:
            next_copy(s_next.at[to], r_prev.at[j], to).start()

    others = pl.ds(0, n_tile - 1)
    all_own = own_copy(s_own.at[others], r_own.at[others], peers[1])
    all_next = next_copy(s_next, r_prev, j)

    r_own[j] = s_own[j]

    win_copy.wait()
    order_copy.wait()
    wp_ref[...] = jnp.dot(order_buf[...], win_buf[...], preferred_element_type=F32).astype(BF16)

    def prepare(e, _):
        w_copy(e).wait()

        def part(n, _):
            rows = pl.ds(pl.multiple_of(n * 32, 32), 32)
            g = [[wbuf[e, a, b, rows].astype(F32) for b in range(3)] for a in range(3)]
            made = time_row_weights(g)
            for i in range(4):
                for jj in range(4):
                    u_ref[e, 4 * i + jj, rows] = made[i][jj].astype(BF16)
            return 0

        lax.fori_loop(0, HID // 32, part, 0)
        return 0

    lax.fori_loop(0, 3, prepare, 0)

    all_own.wait_recv()
    own_ref[...] = r_own[...]

    @pl.when(k > 0)
    def _():
        all_next.wait_recv()
        prev_ref[...] = r_prev[...]

    @pl.when(k == 0)
    def _():
        prev_ref[...] = jnp.zeros_like(prev_ref)

    all_own.wait_send()

    @pl.when(k < last)
    def _():
        all_next.wait_send()


def in_hbm(x):
    return pltpu.with_memory_space_constraint(x, pltpu.HBM)


def in_vmem(x):
    return pltpu.with_memory_space_constraint(x, pltpu.VMEM)


def exchange(n_tm, n_tile, group_frames, latents, win, order, cw):
    vmem = pl.BlockSpec(memory_space=pltpu.VMEM)
    hbm = pl.BlockSpec(memory_space=pltpu.HBM)
    return pl.pallas_call(
        functools.partial(exchange_kernel, n_tm, n_tile),
        out_shape=(
            pltpu.VMEM((LC, FRAMES * WIN, W), BF16),
            pltpu.VMEM((LC, BACK * WIN, W), BF16),
            pltpu.VMEM((3, 16, HID, OUT), BF16),
            pltpu.VMEM((512, HID), BF16),
        ),
        in_specs=[pl.BlockSpec(memory_space=pltpu.SMEM), hbm, hbm, hbm, hbm],
        out_specs=(vmem, vmem, vmem, vmem),
        scratch_shapes=[
            pltpu.VMEM((FRAMES, H, W), BF16),
            pltpu.VMEM((27 * LC, HID), BF16),
            pltpu.VMEM((512, 27 * LC), BF16),
            pltpu.VMEM((BACK + FRAMES, H + 8, W), F32),
            pltpu.VMEM((n_tile, FRAMES * WIN, W), BF16),
            pltpu.VMEM((n_tile, BACK * WIN, W), BF16),
            pltpu.VMEM((LC, FRAMES * WIN, W), BF16),
            pltpu.VMEM((LC, BACK * WIN, W), BF16),
            pltpu.VMEM((3, 3, 3, HID, OUT), BF16),
            pltpu.SemaphoreType.DMA((2,)),
            pltpu.SemaphoreType.DMA((2,)),
            pltpu.SemaphoreType.DMA((3,)),
            pltpu.SemaphoreType.DMA((3,)),
        ],
        compiler_params=pltpu.CompilerParams(
            collective_id=0, has_side_effects=True, vmem_limit_bytes=20 << 20
        ),
        name="exchange",
    )(group_frames, in_hbm(latents), in_hbm(win), in_hbm(order), in_hbm(cw))


def block_kernel(n_tile, gf_ref, own_ref, prev_ref, wp_ref, u_ref, short_hbm, bias_hbm, out_ref,
                 main, turned, hid, act, va, vb, staged, short_ref, bias_ref, in_sem, o_sem):
    k, j = lax.axis_index("tm"), lax.axis_index("tile")
    own_len = gf_ref[0]
    short_copy = pltpu.make_async_copy(short_hbm, short_ref, in_sem.at[0])
    bias_copy = pltpu.make_async_copy(bias_hbm, bias_ref, in_sem.at[1])
    short_copy.start()
    bias_copy.start()

    slot = lax.broadcasted_iota(jnp.int32, (128, 128), 1) % 8

    def lanes(x, shift):
        shift = shift % 128
        return pltpu.roll(x, shift, 1) if shift else x

    def spread(f, planes):
        mid = planes.reshape(LC * WIN, W).T
        left = jnp.concatenate([mid[:1], mid[:-1]], 0)
        right = jnp.concatenate([mid[1:], mid[-1:]], 0)
        for r in range(9):
            t2 = lanes(right, 6 - r)
            turned[f, r] = t2.astype(BF16)
            if r < 6:
                taps = jnp.where(slot < 3, lanes(left, -r), jnp.where(slot < 6, lanes(mid, 3 - r), t2))
                main[f, r] = taps.astype(BF16)

    first = own_ref[:, 0:16].astype(F32)[:, :WIN]
    for g in range(2):
        pair = prev_ref[:, 16 * g:16 * g + 16].astype(F32)
        for h in range(2):
            spread(2 * g + h, jnp.where(k == 0, first, pair[:, h * WIN:(h + 1) * WIN]))
    for g in range(3):
        pair = own_ref[:, 16 * g:16 * g + 16].astype(F32)
        for h in range(2):
            spread(BACK + 2 * g + h, pair[:, h * WIN:(h + 1) * WIN])

    low, high = jnp.where(j == 0, 1, 0), jnp.where(j == n_tile - 1, BAND, BAND + 1)

    def row_step(r, _):
        src = jnp.clip(r, low, high)
        for t in range(8):
            rest = jnp.where(slot == 7, turned[t, src + 1].astype(F32),
                             jnp.where(slot == 6, turned[t + 1, src + 2].astype(F32),
                                       turned[t + 2, src + 3].astype(F32))).astype(BF16)
            taps = jnp.concatenate([main[t, src], main[t + 1, src], main[t + 2, src], rest], 1)
            hidden = jnp.dot(taps, wp_ref[...], preferred_element_type=F32).astype(BF16)
            if t >= 2:
                hid[t - 2, r] = hidden
            half = hidden.astype(F32) * 0.5
            act[r, t] = (half + half * jnp.tanh(half)).astype(BF16)
        return 0

    lax.fori_loop(0, 3, lambda i, c: row_step(2 * i + 1, row_step(2 * i, c)), 0)

    def turn_part(tau, rho, to, n):
        rows = pl.ds(n * 16, 16)

        def four(x):
            return x[0] - x[2], x[1] + x[2], x[2] - x[1], x[1] - x[3]

        planes = [[act[2 * rho + b, 2 * tau + a, rows].astype(F32) for a in range(4)] for b in range(4)]
        in_time = [four(planes[b]) for b in range(4)]
        for i in range(4):
            for jj, made in enumerate(four([in_time[b][i] for b in range(4)])):
                to[4 * i + jj, pl.ds(rho * W + n * 16, 16)] = made.astype(BF16)

    PARTS = W // 16

    def part_rows(n):
        return pl.ds(n * 16, 16)

    def tile_step(tau, frm, to):
        total = [[[None, None], [None, None]] for _ in range(2)]
        done = 0
        for e in range(3):
            rows_out = []
            for i in range(4):
                m = []
                for jj in range(4):
                    m.append(jnp.dot(frm[4 * i + jj], u_ref[e, 4 * i + jj], preferred_element_type=F32))
                rows_out.append(((m[1] + m[2]) + m[0], (m[1] - m[2]) - m[3]))
                step = 4 * e + i + 1
                while to is not None and done * 12 < step * 2 * PARTS and done < 2 * PARTS:
                    turn_part(tau + 1, done // PARTS, to, done % PARTS)
                    done += 1
            for q in range(2):
                s = [x[q] for x in rows_out]
                for p, both in enumerate((s[0] + s[1] + s[2], s[1] - s[2] - s[3])):
                    for rho in range(2):
                        y = both[rho * W:(rho + 1) * W]
                        if e == 0:
                            y = jnp.concatenate([y[:1], y[:-1]], 0)
                        if e == 2:
                            y = jnp.concatenate([y[1:], y[-1:]], 0)
                        total[rho][p][q] = y if e == 0 else total[rho][p][q] + y
        for p in range(2):
            t = 2 * tau + p
            for rho in range(2):
                for q in range(2):
                    r = 2 * rho + q
                    y = total[rho][p][q] + jnp.dot(hid[t, 1 + r], short_ref[...], preferred_element_type=F32) + bias_ref[...]
                    staged[t, r] = jnp.where(t < own_len, y, 0.0).astype(BF16)

    def o_copy(tau):
        frames = pl.ds(2 * tau, 2)
        return pltpu.make_async_copy(staged.at[frames], out_ref.at[frames], o_sem.at[tau])

    for n in range(2 * PARTS):
        turn_part(0, n // PARTS, va, n % PARTS)
    short_copy.wait()
    bias_copy.wait()
    for tau in range(3):
        tile_step(tau, (va, vb)[tau % 2], (vb, va, None)[tau])
        o_copy(tau).start()
    for tau in range(3):
        o_copy(tau).wait()


def block(n_tile, group_frames, own, prev, wp, u, short, bias):
    vmem = pl.BlockSpec(memory_space=pltpu.VMEM)
    hbm = pl.BlockSpec(memory_space=pltpu.HBM)
    return pl.pallas_call(
        functools.partial(block_kernel, n_tile),
        out_shape=jax.ShapeDtypeStruct((FRAMES, BAND, W, OUT), BF16),
        in_specs=[pl.BlockSpec(memory_space=pltpu.SMEM), vmem, vmem, vmem, vmem, hbm, hbm],
        out_specs=hbm,
        scratch_shapes=[
            pltpu.VMEM((BACK + FRAMES, 6, 128, 128), BF16),
            pltpu.VMEM((BACK + FRAMES, 9, 128, 128), BF16),
            pltpu.VMEM((FRAMES, 6, W, HID), BF16),
            pltpu.VMEM((6, 8, W, HID), BF16),
            pltpu.VMEM((16, 2 * W, HID), BF16),
            pltpu.VMEM((16, 2 * W, HID), BF16),
            pltpu.VMEM((FRAMES, BAND, W, OUT), BF16),
            pltpu.VMEM((HID, OUT), BF16),
            pltpu.VMEM((1, OUT), F32),
            pltpu.SemaphoreType.DMA((2,)),
            pltpu.SemaphoreType.DMA((3,)),
        ],
        compiler_params=pltpu.CompilerParams(vmem_limit_bytes=50 << 20),
        name="block",
    )(group_frames, in_vmem(own), in_vmem(prev), in_vmem(wp), in_vmem(u), in_hbm(short), in_hbm(bias))


def per_device(n_tm, n_tile, latents, group_frames, conv_in_weight, conv_weight, shortcut_weight, bias_out):
    order = jnp.asarray(in_weight_order(), BF16)
    own, prev, u, wp = exchange(
        n_tm, n_tile, group_frames, latents.reshape(FRAMES, H, W), conv_in_weight.reshape(27 * LC, HID),
        order, conv_weight)
    return block(n_tile, group_frames, own, prev, wp, u, shortcut_weight, bias_out.reshape(1, OUT))


def solution(mesh):
    in_specs = (P("tm", "tile", None, None), P("tm"), P(), P(), P(), P())
    out_specs = P("tm", "tile", None, None)
    return jax.shard_map(
        functools.partial(per_device, mesh.shape["tm"], mesh.shape["tile"]),
        mesh=mesh, in_specs=in_specs, out_specs=out_specs, check_vma=False,
    )
```

```python
import functools

import jax
import jax.numpy as jnp
import numpy as np
from jax import lax
from jax.experimental import pallas as pl
from jax.experimental.pallas import tpu as pltpu
from jax.sharding import PartitionSpec as P

MESH = pl.DeviceIdType.MESH
F32, BF16 = jnp.float32, jnp.bfloat16

FRAMES = 6
BACK = 4
LC, HID, OUT = 16, 512, 256
H, W = 64, 128
BAND = 4
WIN = BAND + 4


def in_weight_order():
    order = np.zeros((512, 27 * LC), np.float32)
    for a in range(3):
        for q in range(LC):
            for s in range(8):
                e, b = divmod(s, 3)
                order[a * 128 + q * 8 + s, ((a * 3 + b) * 3 + e) * LC + q] = 1
            order[384 + q * 8 + a, ((a * 3 + 2) * 3 + 2) * LC + q] = 1
    return order


def time_row_weights(g):
    def three(x0, x1, x2):
        even, odd = 0.5 * (x0 + x2), 0.5 * x1
        return x0, even + odd, even - odd, x2

    columns = [three(g[0][b], g[1][b], g[2][b]) for b in range(3)]
    return [three(columns[0][i], columns[1][i], columns[2][i]) for i in range(4)]


def exchange_kernel(n_tm, n_tile, gf_ref, lat_ref, win_ref, order_ref, cw_ref,
                    own_ref, prev_ref, u_ref, wp_ref,
                    lat_buf, win_buf, order_buf, pad, s_own, s_next, r_own, r_prev, wbuf,
                    send_sem, recv_sem, w_sem, in_sem):
    k, j = lax.axis_index("tm"), lax.axis_index("tile")
    last = n_tm - 1
    barrier = pltpu.get_barrier_semaphore()

    lat_copy = pltpu.make_async_copy(lat_ref, lat_buf, in_sem.at[0])
    win_copy = pltpu.make_async_copy(win_ref, win_buf, in_sem.at[1])
    order_copy = pltpu.make_async_copy(order_ref, order_buf, in_sem.at[2])
    lat_copy.start()

    def greet(to):
        pl.semaphore_signal(barrier, inc=1, device_id=to, device_id_type=MESH)

    peers = [lax.rem(j + s, n_tile) for s in range(n_tile)]
    for to in peers[1:]:
        greet({"tile": to})

    @pl.when(k > 0)
    def _():
        for to in peers:
            greet({"tm": k - 1, "tile": to})

    def w_copy(e):
        return pltpu.make_async_copy(cw_ref.at[:, :, e], wbuf.at[e], w_sem.at[e])

    win_copy.start()
    order_copy.start()
    for e in range(3):
        w_copy(e).start()

    lat_copy.wait()
    lat = lat_buf[...].astype(F32)
    pad[BACK:, 2:H + 2] = lat
    for row in (0, 1):
        pad[BACK:, row:row + 1] = lat[:, :1]
        pad[BACK:, H + 2 + row:H + 3 + row] = lat[:, H - 1:]
    start = jnp.clip(gf_ref[0] - BACK, 0, FRAMES - BACK) + BACK
    for f in range(BACK):
        pad[f] = pad[start + f]
    for i in range(n_tile):
        rows = pad[:, BAND * i:BAND * i + WIN]
        s_next[i] = rows[:BACK].reshape(BACK * WIN, W).astype(BF16)
        s_own[i] = rows[BACK:].reshape(FRAMES * WIN, W).astype(BF16)

    pl.semaphore_wait(barrier, n_tile - 1 + jnp.where(k < last, n_tile, 0))

    def own_copy(src, dst, to):
        return pltpu.make_async_remote_copy(
            src_ref=src, dst_ref=dst, send_sem=send_sem.at[0], recv_sem=recv_sem.at[0],
            device_id={"tile": to}, device_id_type=MESH)

    def next_copy(src, dst, to):
        return pltpu.make_async_remote_copy(
            src_ref=src, dst_ref=dst, send_sem=send_sem.at[1], recv_sem=recv_sem.at[1],
            device_id={"tm": k + 1, "tile": to}, device_id_type=MESH)

    for to in peers[1:]:
        own_copy(s_own.at[to], r_own.at[j], to).start()

    @pl.when(k < last)
    def _():
        for to in peers:
            next_copy(s_next.at[to], r_prev.at[j], to).start()

    others = pl.ds(0, n_tile - 1)
    all_own = own_copy(s_own.at[others], r_own.at[others], peers[1])
    all_next = next_copy(s_next, r_prev, j)

    r_own[j] = s_own[j]

    win_copy.wait()
    order_copy.wait()
    wp_ref[...] = jnp.dot(order_buf[...], win_buf[...], preferred_element_type=F32).astype(BF16)

    def prepare(e, _):
        w_copy(e).wait()

        def part(n, _):
            rows = pl.ds(pl.multiple_of(n * 32, 32), 32)
            g = [[wbuf[e, a, b, rows].astype(F32) for b in range(3)] for a in range(3)]
            made = time_row_weights(g)
            for i in range(4):
                for jj in range(4):
                    u_ref[e, 4 * i + jj, rows] = made[i][jj].astype(BF16)
            return 0

        lax.fori_loop(0, HID // 32, part, 0)
        return 0

    lax.fori_loop(0, 3, prepare, 0)

    all_own.wait_recv()
    own_ref[...] = r_own[...]

    @pl.when(k > 0)
    def _():
        all_next.wait_recv()
        prev_ref[...] = r_prev[...]

    @pl.when(k == 0)
    def _():
        prev_ref[...] = jnp.zeros_like(prev_ref)

    all_own.wait_send()

    @pl.when(k < last)
    def _():
        all_next.wait_send()


def in_hbm(x):
    return pltpu.with_memory_space_constraint(x, pltpu.HBM)


def in_vmem(x):
    return pltpu.with_memory_space_constraint(x, pltpu.VMEM)


def exchange(n_tm, n_tile, group_frames, latents, win, order, cw):
    vmem = pl.BlockSpec(memory_space=pltpu.VMEM)
    hbm = pl.BlockSpec(memory_space=pltpu.HBM)
    return pl.pallas_call(
        functools.partial(exchange_kernel, n_tm, n_tile),
        out_shape=(
            pltpu.VMEM((LC, FRAMES * WIN, W), BF16),
            pltpu.VMEM((LC, BACK * WIN, W), BF16),
            pltpu.VMEM((3, 16, HID, OUT), BF16),
            pltpu.VMEM((512, HID), BF16),
        ),
        in_specs=[pl.BlockSpec(memory_space=pltpu.SMEM), hbm, hbm, hbm, hbm],
        out_specs=(vmem, vmem, vmem, vmem),
        scratch_shapes=[
            pltpu.VMEM((FRAMES, H, W), BF16),
            pltpu.VMEM((27 * LC, HID), BF16),
            pltpu.VMEM((512, 27 * LC), BF16),
            pltpu.VMEM((BACK + FRAMES, H + 8, W), F32),
            pltpu.VMEM((n_tile, FRAMES * WIN, W), BF16),
            pltpu.VMEM((n_tile, BACK * WIN, W), BF16),
            pltpu.VMEM((LC, FRAMES * WIN, W), BF16),
            pltpu.VMEM((LC, BACK * WIN, W), BF16),
            pltpu.VMEM((3, 3, 3, HID, OUT), BF16),
            pltpu.SemaphoreType.DMA((2,)),
            pltpu.SemaphoreType.DMA((2,)),
            pltpu.SemaphoreType.DMA((3,)),
            pltpu.SemaphoreType.DMA((3,)),
        ],
        compiler_params=pltpu.CompilerParams(
            collective_id=0, has_side_effects=True, vmem_limit_bytes=20 << 20
        ),
        name="exchange",
    )(group_frames, in_hbm(latents), in_hbm(win), in_hbm(order), in_hbm(cw))


def block_kernel(n_tile, gf_ref, own_ref, prev_ref, wp_ref, u_ref, short_hbm, bias_hbm, out_ref,
                 main, cols, hid, act, va, vb, staged, short_ref, bias_ref, in_sem, o_sem):
    k, j = lax.axis_index("tm"), lax.axis_index("tile")
    own_len = gf_ref[0]
    short_copy = pltpu.make_async_copy(short_hbm, short_ref, in_sem.at[0])
    bias_copy = pltpu.make_async_copy(bias_hbm, bias_ref, in_sem.at[1])
    short_copy.start()
    bias_copy.start()

    slot = lax.broadcasted_iota(jnp.int32, (128, 128), 1) % 8

    def lanes(x, shift):
        if isinstance(shift, int):
            shift = shift % 128
            return pltpu.roll(x, shift, 1) if shift else x
        return pltpu.roll(x, lax.rem(shift + 128, 128), 1)

    def columns_first(f):
        if f < BACK:
            pair = prev_ref[:, 16 * (f // 2):16 * (f // 2) + 16].astype(F32)
            first = own_ref[:, 0:16].astype(F32)[:, :WIN]
            planes = jnp.where(k == 0, first, pair[:, f % 2 * WIN:(f % 2 + 1) * WIN])
        else:
            g, h = divmod(f - BACK, 2)
            planes = own_ref[:, 16 * g:16 * g + 16].astype(F32)[:, h * WIN:(h + 1) * WIN]
        mid = planes.reshape(LC * WIN, W).T
        cols[f, 0] = jnp.concatenate([mid[:1], mid[:-1]], 0)
        cols[f, 1] = mid
        cols[f, 2] = jnp.concatenate([mid[1:], mid[-1:]], 0)

    source = [jnp.where(j == 0, 1, 0), 1, 2, 3, 4, jnp.where(j == n_tile - 1, BAND, BAND + 1)]

    def fill(f, r):
        at = source[r]
        main[f, r] = jnp.where(slot < 3, lanes(cols[f, 0], -at),
                               jnp.where(slot < 6, lanes(cols[f, 1], 3 - at), lanes(cols[f, 2], 6 - at))).astype(BF16)

    def planes_of(r, ts):
        lhs = []
        for t in ts:
            at = source[r] + 2
            rest = jnp.where(slot == 0, lanes(cols[t, 2], -at),
                             jnp.where(slot == 1, lanes(cols[t + 1, 2], 1 - at), lanes(cols[t + 2, 2], 2 - at)))
            lhs.append(jnp.concatenate([main[t, r], main[t + 1, r], main[t + 2, r], rest.astype(BF16)], 1))
        hidden = jnp.dot(jnp.concatenate(lhs, 0), wp_ref[...], preferred_element_type=F32).astype(BF16)
        half = hidden.astype(F32) * 0.5
        made = (half + half * jnp.tanh(half)).astype(BF16)
        for n, t in enumerate(ts):
            if t >= 2 and 1 <= r <= BAND:
                hid[t - 2, r - 1] = hidden[n * W:(n + 1) * W]
            act[r, t] = made[n * W:(n + 1) * W]

    def turn_part(tau, rho, to, n):
        rows = pl.ds(n * 16, 16)

        def four(x):
            return x[0] - x[2], x[1] + x[2], x[2] - x[1], x[1] - x[3]

        planes = [[act[2 * rho + b, 2 * tau + a, rows].astype(F32) for a in range(4)] for b in range(4)]
        in_time = [four(planes[b]) for b in range(4)]
        for i in range(4):
            for jj, made in enumerate(four([in_time[b][i] for b in range(4)])):
                to[4 * i + jj, pl.ds(rho * W + n * 16, 16)] = made.astype(BF16)

    PARTS = W // 16

    def part_rows(n):
        return pl.ds(n * 16, 16)

    def tile_step(tau, frm, to):
        base = jnp.dot(hid[2 * tau:2 * tau + 2].reshape(2 * BAND * W, HID), short_ref[...], preferred_element_type=F32)
        base = base + bias_ref[...]
        total = [[[base[((p * 2 + rho) * 2 + q) * W:((p * 2 + rho) * 2 + q + 1) * W] for q in range(2)]
                  for rho in range(2)] for p in range(2)]
        done = dots = 0
        for e in (0, 2, 1):
            rows_out = []
            for i in range(4):
                m = []
                for jj in range(4):
                    m.append(jnp.dot(frm[4 * i + jj], u_ref[e, 4 * i + jj], preferred_element_type=F32))
                    dots += 1
                    while to is not None and done * 48 < dots * 2 * PARTS:
                        turn_part(tau + 1, done // PARTS, to, done % PARTS)
                        done += 1
                rows_out.append(((m[1] + m[2]) + m[0], (m[1] - m[2]) - m[3]))
            for q in range(2):
                s = [x[q] for x in rows_out]
                for p, both in enumerate((s[0] + s[1] + s[2], s[1] - s[2] - s[3])):
                    for rho in range(2):
                        y = both[rho * W:(rho + 1) * W]
                        if e == 0:
                            y = jnp.concatenate([y[:1], y[:-1]], 0)
                        if e == 2:
                            y = jnp.concatenate([y[1:], y[-1:]], 0)
                        total[p][rho][q] = total[p][rho][q] + y
        for p in range(2):
            t = 2 * tau + p
            for rho in range(2):
                for q in range(2):
                    staged[t, 2 * rho + q] = jnp.where(t < own_len, total[p][rho][q], 0.0).astype(BF16)
            o_copy(t).start()

    def o_copy(t):
        return pltpu.make_async_copy(staged.at[t], out_ref.at[t], o_sem.at[t])

    for f in range(6):
        columns_first(f)
    for r in range(6):
        for f in range(6):
            fill(f, r)
        planes_of(r, (0, 1, 2, 3))
        if r < 4:
            columns_first(6 + r)
    for r in range(6):
        fill(6, r)
        fill(7, r)
        planes_of(r, (4, 5))
        for n in range(2 * PARTS * r // 6, 2 * PARTS * (r + 1) // 6):
            turn_part(0, n // PARTS, va, n % PARTS)
    for r in range(6):
        fill(8, r)
        fill(9, r)
        planes_of(r, (6, 7))
    short_copy.wait()
    bias_copy.wait()
    for tau in range(3):
        tile_step(tau, (va, vb)[tau % 2], (vb, va, None)[tau])
    for t in range(FRAMES):
        o_copy(t).wait()


def block(n_tile, group_frames, own, prev, wp, u, short, bias):
    vmem = pl.BlockSpec(memory_space=pltpu.VMEM)
    hbm = pl.BlockSpec(memory_space=pltpu.HBM)
    return pl.pallas_call(
        functools.partial(block_kernel, n_tile),
        out_shape=jax.ShapeDtypeStruct((FRAMES, BAND, W, OUT), BF16),
        in_specs=[pl.BlockSpec(memory_space=pltpu.SMEM), vmem, vmem, vmem, vmem, hbm, hbm],
        out_specs=hbm,
        scratch_shapes=[
            pltpu.VMEM((BACK + FRAMES, 6, 128, 128), BF16),
            pltpu.VMEM((BACK + FRAMES, 3, 128, 128), F32),
            pltpu.VMEM((FRAMES, BAND, W, HID), BF16),
            pltpu.VMEM((6, 8, W, HID), BF16),
            pltpu.VMEM((16, 2 * W, HID), BF16),
            pltpu.VMEM((16, 2 * W, HID), BF16),
            pltpu.VMEM((FRAMES, BAND, W, OUT), BF16),
            pltpu.VMEM((HID, OUT), BF16),
            pltpu.VMEM((1, OUT), F32),
            pltpu.SemaphoreType.DMA((2,)),
            pltpu.SemaphoreType.DMA((FRAMES,)),
        ],
        compiler_params=pltpu.CompilerParams(vmem_limit_bytes=50 << 20),
        name="block",
    )(group_frames, in_vmem(own), in_vmem(prev), in_vmem(wp), in_vmem(u), in_hbm(short), in_hbm(bias))


def per_device(n_tm, n_tile, latents, group_frames, conv_in_weight, conv_weight, shortcut_weight, bias_out):
    order = jnp.asarray(in_weight_order(), BF16)
    own, prev, u, wp = exchange(
        n_tm, n_tile, group_frames, latents.reshape(FRAMES, H, W), conv_in_weight.reshape(27 * LC, HID),
        order, conv_weight)
    return block(n_tile, group_frames, own, prev, wp, u, shortcut_weight, bias_out.reshape(1, OUT))


def solution(mesh):
    in_specs = (P("tm", "tile", None, None), P("tm"), P(), P(), P(), P())
    out_specs = P("tm", "tile", None, None)
    return jax.shard_map(
        functools.partial(per_device, mesh.shape["tm"], mesh.shape["tile"]),
        mesh=mesh, in_specs=in_specs, out_specs=out_specs, check_vma=False,
    )
```

```python
import functools

import jax
import jax.numpy as jnp
import numpy as np
from jax import lax
from jax.experimental import pallas as pl
from jax.experimental.pallas import tpu as pltpu
from jax.sharding import PartitionSpec as P

MESH = pl.DeviceIdType.MESH
F32, BF16 = jnp.float32, jnp.bfloat16

FRAMES = 6
BACK = 4
LC, HID, OUT = 16, 512, 256
H, W = 64, 128
BAND = 4
WIN = BAND + 4


def in_weight_order():
    order = np.zeros((512, 27 * LC), np.float32)
    for a in range(3):
        for q in range(LC):
            for s in range(8):
                e, b = divmod(s, 3)
                order[a * 128 + q * 8 + s, ((a * 3 + b) * 3 + e) * LC + q] = 1
            order[384 + q * 8 + a, ((a * 3 + 2) * 3 + 2) * LC + q] = 1
    return order


def time_row_weights(g):
    def three(x0, x1, x2):
        even, odd = 0.5 * (x0 + x2), 0.5 * x1
        return x0, even + odd, even - odd, x2

    columns = [three(g[0][b], g[1][b], g[2][b]) for b in range(3)]
    return [three(columns[0][i], columns[1][i], columns[2][i]) for i in range(4)]


def exchange_kernel(n_tm, n_tile, gf_ref, lat_ref, win_ref, order_ref, cw_ref,
                    own_ref, prev_ref, u_ref, wp_ref,
                    lat_buf, win_buf, order_buf, pad, s_own, s_next, r_own, r_prev, wbuf,
                    send_sem, recv_sem, w_sem, in_sem):
    k, j = lax.axis_index("tm"), lax.axis_index("tile")
    last = n_tm - 1
    barrier = pltpu.get_barrier_semaphore()

    lat_copy = pltpu.make_async_copy(lat_ref, lat_buf, in_sem.at[0])
    win_copy = pltpu.make_async_copy(win_ref, win_buf, in_sem.at[1])
    order_copy = pltpu.make_async_copy(order_ref, order_buf, in_sem.at[2])
    lat_copy.start()

    def greet(to):
        pl.semaphore_signal(barrier, inc=1, device_id=to, device_id_type=MESH)

    peers = [lax.rem(j + s, n_tile) for s in range(n_tile)]
    for to in peers[1:]:
        greet({"tile": to})

    @pl.when(k > 0)
    def _():
        for to in peers:
            greet({"tm": k - 1, "tile": to})

    def w_copy(e):
        return pltpu.make_async_copy(cw_ref.at[:, :, e], wbuf.at[e], w_sem.at[e])

    win_copy.start()
    order_copy.start()
    for e in range(3):
        w_copy(e).start()

    lat_copy.wait()
    lat = lat_buf[...].astype(F32)
    pad[BACK:, 2:H + 2] = lat
    for row in (0, 1):
        pad[BACK:, row:row + 1] = lat[:, :1]
        pad[BACK:, H + 2 + row:H + 3 + row] = lat[:, H - 1:]
    start = jnp.clip(gf_ref[0] - BACK, 0, FRAMES - BACK) + BACK
    for f in range(BACK):
        pad[f] = pad[start + f]
    for i in range(n_tile):
        rows = pad[:, BAND * i:BAND * i + WIN]
        s_next[i] = rows[:BACK].reshape(BACK * WIN, W).astype(BF16)
        s_own[i] = rows[BACK:].reshape(FRAMES * WIN, W).astype(BF16)

    pl.semaphore_wait(barrier, n_tile - 1 + jnp.where(k < last, n_tile, 0))

    def own_copy(src, dst, to):
        return pltpu.make_async_remote_copy(
            src_ref=src, dst_ref=dst, send_sem=send_sem.at[0], recv_sem=recv_sem.at[0],
            device_id={"tile": to}, device_id_type=MESH)

    def next_copy(src, dst, to):
        return pltpu.make_async_remote_copy(
            src_ref=src, dst_ref=dst, send_sem=send_sem.at[1], recv_sem=recv_sem.at[1],
            device_id={"tm": k + 1, "tile": to}, device_id_type=MESH)

    for s in (10, 6, 9, 11, 14, 2, 8, 5, 7, 13, 15, 1, 3, 4, 12):
        to = peers[s]
        own_copy(s_own.at[to], r_own.at[j], to).start()

    @pl.when(k < last)
    def _():
        for s in (10, 6, 9, 11, 14, 2, 8, 5, 7, 13, 15, 1, 3, 4, 12, 0):
            to = peers[s]
            next_copy(s_next.at[to], r_prev.at[j], to).start()

    others = pl.ds(0, n_tile - 1)
    all_own = own_copy(s_own.at[others], r_own.at[others], peers[1])
    all_next = next_copy(s_next, r_prev, j)

    r_own[j] = s_own[j]

    win_copy.wait()
    order_copy.wait()
    wp_ref[...] = jnp.dot(order_buf[...], win_buf[...], preferred_element_type=F32).astype(BF16)

    def prepare(e, _):
        w_copy(e).wait()

        def part(n, _):
            rows = pl.ds(pl.multiple_of(n * 32, 32), 32)
            g = [[wbuf[e, a, b, rows].astype(F32) for b in range(3)] for a in range(3)]
            made = time_row_weights(g)
            for i in range(4):
                for jj in range(4):
                    u_ref[e, 4 * i + jj, rows] = made[i][jj].astype(BF16)
            return 0

        lax.fori_loop(0, HID // 32, part, 0)
        return 0

    lax.fori_loop(0, 3, prepare, 0)

    all_own.wait_recv()
    own_ref[...] = r_own[...]

    @pl.when(k > 0)
    def _():
        all_next.wait_recv()
        prev_ref[...] = r_prev[...]

    @pl.when(k == 0)
    def _():
        prev_ref[...] = jnp.zeros_like(prev_ref)

    all_own.wait_send()

    @pl.when(k < last)
    def _():
        all_next.wait_send()


def in_hbm(x):
    return pltpu.with_memory_space_constraint(x, pltpu.HBM)


def in_vmem(x):
    return pltpu.with_memory_space_constraint(x, pltpu.VMEM)


def exchange(n_tm, n_tile, group_frames, latents, win, order, cw):
    vmem = pl.BlockSpec(memory_space=pltpu.VMEM)
    hbm = pl.BlockSpec(memory_space=pltpu.HBM)
    return pl.pallas_call(
        functools.partial(exchange_kernel, n_tm, n_tile),
        out_shape=(
            pltpu.VMEM((LC, FRAMES * WIN, W), BF16),
            pltpu.VMEM((LC, BACK * WIN, W), BF16),
            pltpu.VMEM((3, 16, HID, OUT), BF16),
            pltpu.VMEM((512, HID), BF16),
        ),
        in_specs=[pl.BlockSpec(memory_space=pltpu.SMEM), hbm, hbm, hbm, hbm],
        out_specs=(vmem, vmem, vmem, vmem),
        scratch_shapes=[
            pltpu.VMEM((FRAMES, H, W), BF16),
            pltpu.VMEM((27 * LC, HID), BF16),
            pltpu.VMEM((512, 27 * LC), BF16),
            pltpu.VMEM((BACK + FRAMES, H + 8, W), F32),
            pltpu.VMEM((n_tile, FRAMES * WIN, W), BF16),
            pltpu.VMEM((n_tile, BACK * WIN, W), BF16),
            pltpu.VMEM((LC, FRAMES * WIN, W), BF16),
            pltpu.VMEM((LC, BACK * WIN, W), BF16),
            pltpu.VMEM((3, 3, 3, HID, OUT), BF16),
            pltpu.SemaphoreType.DMA((2,)),
            pltpu.SemaphoreType.DMA((2,)),
            pltpu.SemaphoreType.DMA((3,)),
            pltpu.SemaphoreType.DMA((3,)),
        ],
        compiler_params=pltpu.CompilerParams(
            collective_id=0, has_side_effects=True, vmem_limit_bytes=20 << 20
        ),
        name="exchange",
    )(group_frames, in_hbm(latents), in_hbm(win), in_hbm(order), in_hbm(cw))


def block_kernel(n_tile, gf_ref, own_ref, prev_ref, wp_ref, u_ref, short_hbm, bias_hbm, out_ref,
                 main, cols, hid, act, va, vb, staged, short_ref, bias_ref, in_sem, o_sem):
    k, j = lax.axis_index("tm"), lax.axis_index("tile")
    own_len = gf_ref[0]
    short_copy = pltpu.make_async_copy(short_hbm, short_ref, in_sem.at[0])
    bias_copy = pltpu.make_async_copy(bias_hbm, bias_ref, in_sem.at[1])
    short_copy.start()
    bias_copy.start()

    slot = lax.broadcasted_iota(jnp.int32, (128, 128), 1) % 8

    def lanes(x, shift):
        if isinstance(shift, int):
            shift = shift % 128
            return pltpu.roll(x, shift, 1) if shift else x
        return pltpu.roll(x, lax.rem(shift + 128, 128), 1)

    def columns_first(f):
        if f < BACK:
            pair = prev_ref[:, 16 * (f // 2):16 * (f // 2) + 16].astype(F32)
            first = own_ref[:, 0:16].astype(F32)[:, :WIN]
            planes = jnp.where(k == 0, first, pair[:, f % 2 * WIN:(f % 2 + 1) * WIN])
        else:
            g, h = divmod(f - BACK, 2)
            planes = own_ref[:, 16 * g:16 * g + 16].astype(F32)[:, h * WIN:(h + 1) * WIN]
        mid = planes.reshape(LC * WIN, W).T
        cols[f, 0] = jnp.concatenate([mid[:1], mid[:-1]], 0)
        cols[f, 1] = mid
        cols[f, 2] = jnp.concatenate([mid[1:], mid[-1:]], 0)

    source = [jnp.where(j == 0, 1, 0), 1, 2, 3, 4, jnp.where(j == n_tile - 1, BAND, BAND + 1)]

    def fill(f, r):
        at = source[r]
        main[f, r] = jnp.where(slot < 3, lanes(cols[f, 0], -at),
                               jnp.where(slot < 6, lanes(cols[f, 1], 3 - at), lanes(cols[f, 2], 6 - at))).astype(BF16)

    def planes_of(r, ts):
        lhs = []
        for t in ts:
            at = source[r] + 2
            rest = jnp.where(slot == 0, lanes(cols[t, 2], -at),
                             jnp.where(slot == 1, lanes(cols[t + 1, 2], 1 - at), lanes(cols[t + 2, 2], 2 - at)))
            lhs.append(jnp.concatenate([main[t, r], main[t + 1, r], main[t + 2, r], rest.astype(BF16)], 1))
        hidden = jnp.dot(jnp.concatenate(lhs, 0), wp_ref[...], preferred_element_type=F32).astype(BF16)
        half = hidden.astype(F32) * 0.5
        made = (half + half * jnp.tanh(half)).astype(BF16)
        for n, t in enumerate(ts):
            if t >= 2 and 1 <= r <= BAND:
                hid[t - 2, r - 1] = hidden[n * W:(n + 1) * W]
            act[r, t] = made[n * W:(n + 1) * W]

    def turn_part(tau, rho, to, n):
        rows = pl.ds(n * 16, 16)

        def four(x):
            return x[0] - x[2], x[1] + x[2], x[2] - x[1], x[1] - x[3]

        planes = [[act[2 * rho + b, 2 * tau + a, rows].astype(F32) for a in range(4)] for b in range(4)]
        in_time = [four(planes[b]) for b in range(4)]
        for i in range(4):
            for jj, made in enumerate(four([in_time[b][i] for b in range(4)])):
                to[4 * i + jj, pl.ds(rho * W + n * 16, 16)] = made.astype(BF16)

    PARTS = W // 16

    def part_rows(n):
        return pl.ds(n * 16, 16)

    def tile_step(tau, frm, to):
        base = jnp.dot(hid[2 * tau:2 * tau + 2].reshape(2 * BAND * W, HID), short_ref[...], preferred_element_type=F32)
        base = base + bias_ref[...]
        total = [[[base[((p * 2 + rho) * 2 + q) * W:((p * 2 + rho) * 2 + q + 1) * W] for q in range(2)]
                  for rho in range(2)] for p in range(2)]
        done = dots = 0
        for e in (0, 2, 1):
            rows_out = []
            for i in range(4):
                m = []
                for jj in range(4):
                    m.append(jnp.dot(frm[4 * i + jj], u_ref[e, 4 * i + jj], preferred_element_type=F32))
                    dots += 1
                    while to is not None and done * 48 < dots * 2 * PARTS:
                        turn_part(tau + 1, done // PARTS, to, done % PARTS)
                        done += 1
                rows_out.append(((m[1] + m[2]) + m[0], (m[1] - m[2]) - m[3]))
            for q in range(2):
                s = [x[q] for x in rows_out]
                for p, both in enumerate((s[0] + s[1] + s[2], s[1] - s[2] - s[3])):
                    for rho in range(2):
                        y = both[rho * W:(rho + 1) * W]
                        if e == 0:
                            y = jnp.concatenate([y[:1], y[:-1]], 0)
                        if e == 2:
                            y = jnp.concatenate([y[1:], y[-1:]], 0)
                        total[p][rho][q] = total[p][rho][q] + y
        for p in range(2):
            t = 2 * tau + p
            for rho in range(2):
                for q in range(2):
                    staged[t, 2 * rho + q] = jnp.where(t < own_len, total[p][rho][q], 0.0).astype(BF16)
            o_copy(t).start()

    def o_copy(t):
        return pltpu.make_async_copy(staged.at[t], out_ref.at[t], o_sem.at[t])

    for f in range(6):
        columns_first(f)
    for r in range(6):
        for f in range(6):
            fill(f, r)
        planes_of(r, (0, 1, 2, 3))
        if r < 4:
            columns_first(6 + r)
    for r in range(6):
        fill(6, r)
        fill(7, r)
        planes_of(r, (4, 5))
        for n in range(2 * PARTS * r // 6, 2 * PARTS * (r + 1) // 6):
            turn_part(0, n // PARTS, va, n % PARTS)
    for r in range(6):
        fill(8, r)
        fill(9, r)
        planes_of(r, (6, 7))
    short_copy.wait()
    bias_copy.wait()
    for tau in range(3):
        tile_step(tau, (va, vb)[tau % 2], (vb, va, None)[tau])
    for t in range(FRAMES):
        o_copy(t).wait()


def block(n_tile, group_frames, own, prev, wp, u, short, bias):
    vmem = pl.BlockSpec(memory_space=pltpu.VMEM)
    hbm = pl.BlockSpec(memory_space=pltpu.HBM)
    return pl.pallas_call(
        functools.partial(block_kernel, n_tile),
        out_shape=jax.ShapeDtypeStruct((FRAMES, BAND, W, OUT), BF16),
        in_specs=[pl.BlockSpec(memory_space=pltpu.SMEM), vmem, vmem, vmem, vmem, hbm, hbm],
        out_specs=hbm,
        scratch_shapes=[
            pltpu.VMEM((BACK + FRAMES, 6, 128, 128), BF16),
            pltpu.VMEM((BACK + FRAMES, 3, 128, 128), F32),
            pltpu.VMEM((FRAMES, BAND, W, HID), BF16),
            pltpu.VMEM((6, 8, W, HID), BF16),
            pltpu.VMEM((16, 2 * W, HID), BF16),
            pltpu.VMEM((16, 2 * W, HID), BF16),
            pltpu.VMEM((FRAMES, BAND, W, OUT), BF16),
            pltpu.VMEM((HID, OUT), BF16),
            pltpu.VMEM((1, OUT), F32),
            pltpu.SemaphoreType.DMA((2,)),
            pltpu.SemaphoreType.DMA((FRAMES,)),
        ],
        compiler_params=pltpu.CompilerParams(vmem_limit_bytes=50 << 20),
        name="block",
    )(group_frames, in_vmem(own), in_vmem(prev), in_vmem(wp), in_vmem(u), in_hbm(short), in_hbm(bias))


def per_device(n_tm, n_tile, latents, group_frames, conv_in_weight, conv_weight, shortcut_weight, bias_out):
    order = jnp.asarray(in_weight_order(), BF16)
    own, prev, u, wp = exchange(
        n_tm, n_tile, group_frames, latents.reshape(FRAMES, H, W), conv_in_weight.reshape(27 * LC, HID),
        order, conv_weight)
    return block(n_tile, group_frames, own, prev, wp, u, shortcut_weight, bias_out.reshape(1, OUT))


def solution(mesh):
    in_specs = (P("tm", "tile", None, None), P("tm"), P(), P(), P(), P())
    out_specs = P("tm", "tile", None, None)
    return jax.shard_map(
        functools.partial(per_device, mesh.shape["tm"], mesh.shape["tile"]),
        mesh=mesh, in_specs=in_specs, out_specs=out_specs, check_vma=False,
    )
```
